512 devices in a mesh: dp: 16 (over y, z_hi, core), expert: 8 (over z_lo), mp: 4 (over x).
Axes of the slice: x: 4, y: 4, z: 16 (z_hi: 2, z_lo: 8; z = z_hi * 8 + z_lo), core: 2. Of those that a mesh axis runs over, the one named last changes fastest.
Arguments:
- expert_ids: int32 [2048, 2], P('dp'), may hold values from 0 to 7, all different within a row; in each aligned block of 128 rows (0 to 127, 128 to 255, ...) at most 48 rows name the same one
- gate_weights: float32 [2048, 2], P('dp'), may hold values from 0.1 to 1
- hidden: bfloat16 [8, 768, 8192], P('expert', 'mp', 'dp'), may hold values from -6 to 6
- down_weight: bfloat16 [8, 8192, 6144], P('expert', 'dp', 'mp'), may hold values from -0.0625 to 0.0625
- cotangent: bfloat16 [2048, 6144], P('dp', 'mp'), may hold values from -1.5 to 1.5
Outputs:
- mixed: bfloat16 [2048, 6144], P('dp', 'mp')
- gate_grad: float32 [2048, 2], P('dp')
- hidden_grad: bfloat16 [8, 768, 8192], P('expert', 'mp', 'dp')
- weight_grad: bfloat16 [8, 8192, 6144], P('expert', 'dp', 'mp')
The draws below stay inside these ranges and needn't reach their ends.
Inputs may be any that keep to these rules, and one draw needn't show every extreme that they name: `expert_ids`: each row names two different experts. Within the 128 rows of one index of dp, no expert is named more than 48 times, a bound that some block reaches.
All inputs are finite; a program needn't handle non-finite values.
Results may differ from the reference program's by a relative error of at most 0.02.
Values may be sent and summed in bfloat16 or wider, within the bound.
A program may use at most 64 MiB of HBM per device.

```python
import math
import jax
import jax.numpy as jnp
import numpy as np
from jax import lax

D = 6144
H = 8192
TOK_DP = 128
EXPERTS = 8
CAP = 48
TOKENS = 2048
SLOTS = 768
N_DP = 16


def raised(array, own_key, source, target, blocks, factor):
    owner, partner = [(jnp.arange(array.shape[dim]) // (array.shape[dim] // blocks)).reshape([-1 if axis == dim else 1 for axis in range(array.ndim)]) for dim in (source, target)]
    chosen = jax.random.permutation(own_key, blocks)[partner]
    strong = (owner == chosen) | (owner == (partner + blocks // 2) % blocks)
    return jnp.where(strong, factor * array, array)


def steps_of(stream_key, shape, shards, smallest, high):
    factor_of = 1.0
    for axis_at, blocks in shards:
        draws = jax.random.uniform(jax.random.fold_in(jax.random.fold_in(stream_key, 6), axis_at), (blocks,), jnp.float32, smallest / len(shards), high / len(shards))
        factor_of = factor_of * jnp.repeat(jnp.exp(draws), shape[axis_at] // blocks).reshape((-1,) + (1,) * (len(shape) - 1 - axis_at))
    return factor_of


def deal_out(key, own, number, rows, count, top, most, slope):
    order = jax.random.permutation(key, count)
    crowded, ordinary = load_shares(count, rows * top, most, slope, True), load_shares(count, rows * top, most, slope, False)
    places = jnp.arange(count)

    def named(sizes, rotation):
        used = int((sizes > 0).sum())
        fixed = max(1, used // 4)
        moved = fixed + (places - fixed + rotation * (used - fixed)) % max(1, count - fixed)
        return jnp.zeros((count,), jnp.int32).at[order[jnp.where(places < fixed, places, moved)]].set(jnp.asarray(sizes, jnp.int32))

    sizes = jnp.where(number % 4 == 0, named(crowded, number // 4), named(ordinary, number - number // 4 - 1))
    mixed = jax.random.permutation(jax.random.fold_in(own, 3), count)
    donor, receiver = mixed[0:count // 2 * 2:2], mixed[1:count // 2 * 2:2]
    margin = jnp.minimum(sizes[donor] - 1, most - sizes[receiver]) // 2
    margin = jnp.where((donor == order[0]) | (receiver == order[0]) | (sizes[receiver] == 0), 0, jnp.maximum(margin, 0))
    moved = jax.random.randint(jax.random.fold_in(own, 4), (count // 2,), 0, 1 << 20) % (margin + 1)
    sizes = sizes.at[donor].add(-moved).at[receiver].add(moved)
    items = jnp.searchsorted(jnp.cumsum(sizes), jnp.arange(rows * top), side="right").astype(jnp.int32)
    table = items.reshape(top, rows).T
    table = table[jax.random.permutation(jax.random.fold_in(own, 1), rows)]
    rotation = jax.random.randint(jax.random.fold_in(own, 2), (rows, 1), 0, top)
    return jnp.take_along_axis(table, (jnp.arange(top)[None, :] + rotation) % top, axis=1)


def load_shares(amount, total, limit, slope, full):
    portions = [(1 << 20) // math.isqrt(standing ** slope) + 1 for standing in range(1, amount + 1)]
    largest = limit if full else min(limit, max(-(-total // amount), total * portions[0] // sum(portions)))
    least = 1 if total - largest >= amount - 1 else 0
    holding, rest = [largest] + [least] * (amount - 1), total - largest - least * (amount - 1)
    while rest > 0:
        movable = [i for i in range(1, amount) if holding[i] < largest] or [i for i in range(1, amount) if holding[i] < limit]
        mass, left = sum([portions[i] for i in movable]), rest
        for i in movable:
            addition = min(limit - holding[i], max(1, left * portions[i] // mass), rest)
            holding[i] = holding[i] + addition
            rest = rest - addition
    return np.array(holding)


def centred(key, extent, scale, bound, cuts=(), held_as=jnp.bfloat16):
    gain = steps_of(key, extent, cuts, -0.22, 0.18) if cuts else 1.0
    array = jax.random.normal(key, extent, jnp.float32) * scale * gain
    return jnp.minimum(jnp.maximum(array, -bound), bound).astype(held_as)


def gaussian_with(own_key, extent, deviation, limit, pieces, heavy, kind=jnp.bfloat16):
    entries = deviation * jax.random.normal(own_key, extent, jnp.float32)
    if pieces:
        entries = entries * steps_of(own_key, extent, pieces, -0.22, 0.18)
    return jnp.clip(raised(entries, jax.random.fold_in(own_key, 3), *heavy), -limit, limit).astype(kind)


def setup_inputs(seed: int = 0) -> dict:
    seeds = jax.random.split(jax.random.key(seed), 6)
    expert_ids_keys = jax.random.split(jax.random.fold_in(seeds[0], 1), TOKENS // TOK_DP)
    expert_ids_turns = jax.random.permutation(jax.random.fold_in(seeds[0], 3), TOKENS // TOK_DP)
    expert_ids = jax.vmap(lambda own, number: deal_out(jax.random.fold_in(seeds[0], 2), own, number, TOK_DP, EXPERTS, 2, CAP, 2))(expert_ids_keys, expert_ids_turns).reshape((TOKENS, 2))
    gate_weights = jnp.clip(0.1 + 0.9 * jax.random.uniform(seeds[1], (TOKENS, 2), jnp.float32) ** steps_of(seeds[1], (TOKENS, 2), ((0, 16),), -0.2, 0.2), 0.1, 1.0)
    hidden = gaussian_with(seeds[2], (EXPERTS, SLOTS, H), 1.0, 6.0, ((0, 8), (1, 4), (2, 16)), (2, 1, 16, 2.0))
    down_weight = centred(seeds[3], (EXPERTS, H, D), H ** -0.5, 0.0625, ((0, 8), (1, 16), (2, 4)))
    cotangent = centred(seeds[4], (TOKENS, D), 0.25, 1.5, ((0, 16), (1, 4)))
    return dict(expert_ids=expert_ids, gate_weights=gate_weights, hidden=hidden, down_weight=down_weight, cotangent=cotangent)


def slot_of(expert_ids):
    blocks = expert_ids.reshape(N_DP, TOK_DP * 2)
    onehot = (blocks[:, :, None] == jnp.arange(EXPERTS, dtype=jnp.int32)[None, None, :]).astype(jnp.int32)
    before = jnp.cumsum(onehot, axis=1) - onehot
    position = jnp.sum(before * onehot, axis=2)
    slots = position + (jnp.arange(N_DP, dtype=jnp.int32) * CAP)[:, None]
    return slots.reshape(TOKENS, 2).astype(jnp.int32)


def project(pair):
    rows, weight = pair
    row_blocks = rows.reshape(SLOTS, N_DP, H // N_DP).transpose(1, 0, 2)
    weight_blocks = weight.reshape(N_DP, H // N_DP, D)

    def add_block(total, piece):
        part = jnp.dot(piece[0], piece[1], preferred_element_type=jnp.float32).astype(jnp.bfloat16)
        part = lax.optimization_barrier(part)
        return total + part.astype(jnp.float32), None

    total, unused = lax.scan(add_block, jnp.zeros((SLOTS, D), jnp.float32), (row_blocks, weight_blocks))
    return total.astype(jnp.bfloat16)


def back_hidden(pair):
    return jnp.dot(pair[0], pair[1].T, preferred_element_type=jnp.float32).astype(jnp.bfloat16)


def back_weight(pair):
    return jnp.dot(pair[0].T, pair[1], preferred_element_type=jnp.float32).astype(jnp.bfloat16)


def reference(expert_ids, gate_weights, hidden, down_weight, cotangent):
    slots = slot_of(expert_ids)
    out = lax.map(project, (hidden, down_weight))
    rows = out[expert_ids, slots].astype(jnp.float32)
    cot_f32 = cotangent.astype(jnp.float32)
    mixed = jnp.sum(gate_weights[:, :, None] * rows, axis=1).astype(jnp.bfloat16)
    gate_grad = jnp.sum(rows * cot_f32[:, None, :], axis=2)
    scaled = (gate_weights[:, :, None] * cot_f32[:, None, :]).astype(jnp.bfloat16)
    slot_cotangent = jnp.zeros((EXPERTS, SLOTS, D), jnp.bfloat16).at[expert_ids, slots].set(scaled)
    hidden_grad = lax.map(back_hidden, (slot_cotangent, down_weight))
    weight_grad = lax.map(back_weight, (hidden, slot_cotangent))
    return mixed, gate_grad, hidden_grad, weight_grad
```

```python
import jax
import jax.numpy as jnp
from jax import lax
from jax.experimental import pallas as pl
from jax.experimental.pallas import tpu as pltpu
from jax.sharding import PartitionSpec as P

MESH = pl.DeviceIdType.MESH
F32 = jnp.float32
BF16 = jnp.bfloat16
NT = (((1,), (1,)), ((), ()))
TN = (((0,), (0,)), ((), ()))

NX, NY, NE = 4, 4, 8
CAP, ROWS, DEPTH, COLS, TOKS = 48, 192, 512, 1536, 128
GROUPS = 3
WIDE = COLS // GROUPS
LANES = 128
CHUNKS = COLS // LANES
PER_GROUP = WIDE // LANES
STEPS = CHUNKS + NE - 1


def kernel(
    ids_ref, gates_ref, hidden_ref, weight_ref, cot_ref,
    mixed_ref, gate_ref, hgrad_ref, wgrad_ref,
    hid_all, slot_all, cot_sel, parts, core_rx, core_sum, y_rx, z_own, z_tx, z_rx,
    tok, up_tx, up_rx, down_tx, down_rx, hg_tx, hg_rx, gate_tx, gate_sum, gate_xrx, gate_erx, gate_acc,
    hid_sem, slot_z_sem, slot_y_sem, slot_c_sem, core_sem, y_sem, z_sem, up_sem, down_sem, hg_sem, gx_sem, ge_sem,
):
    dp = lax.axis_index("dp")
    ex = lax.axis_index("expert")
    mx = lax.axis_index("mp")
    core = dp % 2
    half = (dp // 2) % 2
    row = dp // 4

    def dp_of(y, h, c):
        return (y * 2 + h) * 2 + c

    def x_peer(d):
        return {"mp": (mx + d) % NX}

    def y_peer(d):
        return {"dp": dp_of((row + d) % NY, half, core)}

    def e_peer(d):
        return {"expert": (ex + d) % NE}

    core_peer = {"dp": dp_of(row, half, 1 - core)}
    half_peer = {"dp": dp_of(row, 1 - half, core)}

    def remote(src, dst, sems, index, peer):
        return pltpu.make_async_remote_copy(
            src_ref=src,
            dst_ref=dst,
            send_sem=sems.at[(0, *index)],
            recv_sem=sems.at[(1, *index)],
            device_id=peer,
            device_id_type=MESH,
        )

    barrier = pltpu.get_barrier_semaphore()
    peers = [x_peer(d) for d in range(1, NX)] + [y_peer(d) for d in range(1, NY)]
    peers += [e_peer(d) for d in range(1, NE)] + [core_peer, half_peer]
    for peer in peers:
        pl.semaphore_signal(barrier, inc=1, device_id=peer, device_id_type=MESH)

    hit0 = (ids_ref[0:1, :] == ex).astype(F32)
    hit1 = (ids_ref[1:2, :] == ex).astype(F32)
    hits = hit0 + hit1
    gate_of = hit0 * gates_ref[0:1, :] + hit1 * gates_ref[1:2, :]
    earlier = lax.broadcasted_iota(jnp.int32, (TOKS, TOKS), 0) < lax.broadcasted_iota(
        jnp.int32, (TOKS, TOKS), 1
    )
    place = jnp.dot(
        jnp.broadcast_to(hits, (16, TOKS)).astype(BF16),
        earlier.astype(F32).astype(BF16),
        preferred_element_type=F32,
    )[0:1, :]
    slot = lax.broadcasted_iota(jnp.int32, (CAP, TOKS), 0).astype(F32)
    sel = jnp.where(slot == place, jnp.broadcast_to(hits, (CAP, TOKS)), 0.0)
    slot_gate = jnp.sum(sel * gate_of, axis=1, keepdims=True)
    sel16 = sel.astype(BF16)
    picked = jnp.dot(sel16, cot_ref[...], preferred_element_type=F32)
    cot_sel[...] = picked
    slot_all[dp] = (slot_gate * picked).astype(BF16)
    hid_all[mx] = hidden_ref[...]
    gate_acc[...] = jnp.zeros_like(gate_acc)

    pl.semaphore_wait(barrier, len(peers))

    hid_copies = [
        remote(hidden_ref, hid_all.at[mx], hid_sem, (d - 1,), x_peer(d)) for d in (1, 3, 2)
    ]
    for copy in hid_copies:
        copy.start()

    def slot_y(side, block):
        return [
            remote(slot_all.at[block], slot_all.at[block], slot_y_sem, (side, d - 1), y_peer(d))
            for d in (1, 3, 2)
        ]

    def slot_core(index, block):
        return remote(slot_all.at[block], slot_all.at[block], slot_c_sem, (index,), core_peer)

    other_block = dp_of(row, 1 - half, core)
    slot_z = remote(slot_all.at[dp], slot_all.at[dp], slot_z_sem, (0,), half_peer)
    slot_z.start()
    own_y = slot_y(0, dp)
    for copy in own_y:
        copy.start()
    core_copies = [slot_core(0, dp)]
    core_copies[0].start()

    for copy in hid_copies:
        copy.wait_recv()
    rows_all = hid_all[...].reshape(NX * ROWS, DEPTH)
    to_core = []
    for g in range(GROUPS):
        product = jnp.dot(
            rows_all, weight_ref[:, g * WIDE : (g + 1) * WIDE], preferred_element_type=F32
        ).astype(BF16)
        product = product.reshape(NY, 2, 2, CAP, WIDE)
        for c in range(2):
            parts[g, c] = product[:, :, c]
        copy = remote(parts.at[g, 1 - core], core_rx.at[g], core_sem, (g,), core_peer)
        copy.start()
        to_core.append(copy)

    to_y = []
    for g in range(GROUPS):
        to_core[g].wait_recv()
        core_sum[g] = (parts[g, core].astype(F32) + core_rx[g].astype(F32)).astype(BF16)
        group = []
        for d in (2, 1, 3):
            copy = remote(
                core_sum.at[g, (row + d) % NY], y_rx.at[g, d - 1], y_sem, (g, d - 1), y_peer(d)
            )
            copy.start()
            group.append(copy)
        to_y.append(group)

    for n, copy in enumerate(own_y):
        copy.wait_recv()
        d = (1, 3, 2)[n]
        onward = slot_core(1 + n, dp_of((row - d + NY) % NY, half, core))
        onward.start()
        core_copies.append(onward)
    slot_z.wait_recv()
    other_y = slot_y(1, other_block)
    for copy in other_y:
        copy.start()
    onward = slot_core(4, other_block)
    onward.start()
    core_copies.append(onward)

    to_z = []
    for g in range(GROUPS):
        for copy in to_y[g]:
            copy.wait_recv()
        mine = core_sum[g, row].astype(F32)
        for d in range(1, NY):
            mine = mine + y_rx[g, d - 1].astype(F32)
        z_own[g] = mine
        z_tx[g] = z_own[g, 1 - half].astype(BF16)
        copy = remote(z_tx.at[g], z_rx.at[g], z_sem, (g,), half_peer)
        copy.start()
        to_z.append(copy)

    for n, copy in enumerate(other_y):
        copy.wait_recv()
        d = (1, 3, 2)[n]
        onward = slot_core(5 + n, dp_of((row - d + NY) % NY, 1 - half, core))
        onward.start()
        core_copies.append(onward)
    for copy in core_copies:
        copy.wait_recv()

    slots = slot_all[...].reshape(NX * ROWS, COLS)
    hg_tx[...] = (
        lax.dot_general(slots, weight_ref[...], NT, preferred_element_type=F32)
        .astype(BF16)
        .reshape(NX, ROWS, DEPTH)
    )
    hg_copies = [
        remote(hg_tx.at[(mx + d) % NX], hg_rx.at[d - 1], hg_sem, (d - 1,), x_peer(d))
        for d in (2, 1, 3)
    ]
    for copy in hg_copies:
        copy.start()
    rows_t = hid_all[...].reshape(NX * ROWS, DEPTH).T
    for g in range(GROUPS):
        wgrad_ref[:, g * WIDE : (g + 1) * WIDE] = jnp.dot(
            rows_t,
            slot_all[:, :, g * WIDE : (g + 1) * WIDE].reshape(NX * ROWS, WIDE),
            preferred_element_type=F32,
        ).astype(BF16)

    sel_t = sel.T.astype(BF16)

    def take_group(g):
        remote(z_tx.at[g], z_rx.at[g], z_sem, (g,), half_peer).wait_recv()
        out = (z_own[g, half] + z_rx[g].astype(F32)).astype(BF16).astype(F32)
        for n in range(GROUPS):

            @pl.when(g == n)
            def _():
                dots = out * cot_sel[:, n * WIDE : (n + 1) * WIDE]
                gate_acc[...] += jnp.sum(dots, axis=1, keepdims=True)

        weighted = jnp.dot(
            sel_t, (slot_gate * out).astype(BF16), preferred_element_type=F32
        ).astype(BF16)
        for n in range(PER_GROUP):
            tok[g * PER_GROUP + n] = weighted[:, n * LANES : (n + 1) * LANES]

    up_peer, down_peer = e_peer(1), e_peer(NE - 1)

    def up_copy(q):
        return remote(up_tx.at[q], up_rx.at[q], up_sem, (q,), up_peer)

    def down_copy(q):
        return remote(down_tx.at[q], down_rx.at[q], down_sem, (q,), down_peer)

    gate_x = [remote(gate_tx, gate_xrx.at[d - 1], gx_sem, (d - 1,), x_peer(d)) for d in (2, 1, 3)]
    gate_e = [
        remote(gate_sum, gate_erx.at[d - 1], ge_sem, (d - 1,), e_peer(d)) for d in range(1, NE)
    ]

    def step(s, carry):
        @pl.when(jnp.logical_and(s % PER_GROUP == 0, s < CHUNKS))
        def _():
            take_group(s // PER_GROUP)

        @pl.when(s == CHUNKS - 1)
        def _():
            per_token = jnp.sum(sel * gate_acc[:, 0:1], axis=0, keepdims=True)
            gate_tx[...] = jnp.zeros_like(gate_tx)
            gate_tx[0:1, :] = per_token * hit0
            gate_tx[1:2, :] = per_token * hit1
            for copy in gate_x:
                copy.start()

        @pl.when(s == CHUNKS + 2)
        def _():
            for copy in gate_x:
                copy.wait_recv()
            gate_sum[...] = gate_tx[...] + gate_xrx[0] + gate_xrx[1] + gate_xrx[2]
            for copy in gate_e:
                copy.start()

        q = s - ex

        @pl.when(jnp.logical_and(q >= 0, q < CHUNKS))
        def _():
            @pl.when(ex == 0)
            def _():
                up_tx[q] = tok[q]

            @pl.when(ex > 0)
            def _():
                up_copy(q).wait_recv()
                up_tx[q] = (tok[q].astype(F32) + up_rx[q].astype(F32)).astype(BF16)

            @pl.when(ex < NE - 1)
            def _():
                up_copy(q).start()

        r = s - (NE - 1 - ex)

        @pl.when(jnp.logical_and(r >= 0, r < CHUNKS))
        def _():
            @pl.when(ex == NE - 1)
            def _():
                down_tx[r] = tok[r]

            @pl.when(ex < NE - 1)
            def _():
                down_copy(r).wait_recv()
                down_tx[r] = (tok[r].astype(F32) + down_rx[r].astype(F32)).astype(BF16)

            @pl.when(ex > 0)
            def _():
                down_copy(r).start()

        return carry

    lax.fori_loop(0, STEPS, step, 0)

    for q in range(CHUNKS):
        columns = slice(q * LANES, (q + 1) * LANES)

        @pl.when(ex < NE - 1)
        def _():
            mixed_ref[:, columns] = (up_tx[q].astype(F32) + down_rx[q].astype(F32)).astype(BF16)

        @pl.when(ex == NE - 1)
        def _():
            mixed_ref[:, columns] = up_tx[q]

    for copy in hg_copies:
        copy.wait_recv()
    total = hg_tx[mx].astype(F32)
    for d in range(1, NX):
        total = total + hg_rx[d - 1].astype(F32)
    hgrad_ref[...] = total.astype(BF16)

    for copy in gate_e:
        copy.wait_recv()
    gates = gate_sum[...]
    for d in range(1, NE):
        gates = gates + gate_erx[d - 1]
    gate_ref[...] = gates

    for copy in [*hid_copies, slot_z, *own_y, *other_y, *core_copies, *to_core, *to_z]:
        copy.wait_send()
    for group in to_y:
        for copy in group:
            copy.wait_send()
    for copy in [*hg_copies, *gate_x, *gate_e]:
        copy.wait_send()

    def drain(q, carry):
        @pl.when(ex < NE - 1)
        def _():
            up_copy(q).wait_send()

        @pl.when(ex > 0)
        def _():
            down_copy(q).wait_send()

        return carry

    lax.fori_loop(0, CHUNKS, drain, 0)


def body(expert_ids, gate_weights, hidden, down_weight, cotangent):
    vmem = pl.BlockSpec(memory_space=pltpu.VMEM)
    dma = pltpu.SemaphoreType.DMA
    mixed, gates, hgrad, wgrad = pl.pallas_call(
        kernel,
        name="layer",
        out_shape=(
            jax.ShapeDtypeStruct((TOKS, COLS), BF16),
            jax.ShapeDtypeStruct((8, TOKS), F32),
            jax.ShapeDtypeStruct((ROWS, DEPTH), BF16),
            jax.ShapeDtypeStruct((DEPTH, COLS), BF16),
        ),
        in_specs=[vmem] * 5,
        out_specs=(vmem,) * 4,
        scratch_shapes=[
            pltpu.VMEM((NX, ROWS, DEPTH), BF16),
            pltpu.VMEM((16, CAP, COLS), BF16),
            pltpu.VMEM((CAP, COLS), F32),
            pltpu.VMEM((GROUPS, 2, NY, 2, CAP, WIDE), BF16),
            pltpu.VMEM((GROUPS, NY, 2, CAP, WIDE), BF16),
            pltpu.VMEM((GROUPS, NY, 2, CAP, WIDE), BF16),
            pltpu.VMEM((GROUPS, NY - 1, 2, CAP, WIDE), BF16),
            pltpu.VMEM((GROUPS, 2, CAP, WIDE), F32),
            pltpu.VMEM((GROUPS, CAP, WIDE), BF16),
            pltpu.VMEM((GROUPS, CAP, WIDE), BF16),
            pltpu.VMEM((CHUNKS, TOKS, LANES), BF16),
            pltpu.VMEM((CHUNKS, TOKS, LANES), BF16),
            pltpu.VMEM((CHUNKS, TOKS, LANES), BF16),
            pltpu.VMEM((CHUNKS, TOKS, LANES), BF16),
            pltpu.VMEM((CHUNKS, TOKS, LANES), BF16),
            pltpu.VMEM((NX, ROWS, DEPTH), BF16),
            pltpu.VMEM((NX - 1, ROWS, DEPTH), BF16),
            pltpu.VMEM((8, TOKS), F32),
            pltpu.VMEM((8, TOKS), F32),
            pltpu.VMEM((NX - 1, 8, TOKS), F32),
            pltpu.VMEM((NE - 1, 8, TOKS), F32),
            pltpu.VMEM((CAP, TOKS), F32),
            dma((2, NX - 1)),
            dma((2, 1)),
            dma((2, 2, NY - 1)),
            dma((2, 8)),
            dma((2, GROUPS)),
            dma((2, GROUPS, NY - 1)),
            dma((2, GROUPS)),
            dma((2, CHUNKS)),
            dma((2, CHUNKS)),
            dma((2, NX - 1)),
            dma((2, NX - 1)),
            dma((2, NE - 1)),
        ],
        compiler_params=pltpu.CompilerParams(
            collective_id=0, has_side_effects=True, vmem_limit_bytes=50 * 2**20
        ),
    )(expert_ids.T, gate_weights.T, hidden[0], down_weight[0], cotangent)
    return mixed, gates[0:2].T, hgrad[None], wgrad[None]


def solution(mesh):
    in_specs = (
        P("dp", None),
        P("dp", None),
        P("expert", "mp", "dp"),
        P("expert", "dp", "mp"),
        P("dp", "mp"),
    )
    out_specs = (P("dp", "mp"), P("dp", None), P("expert", "mp", "dp"), P("expert", "dp", "mp"))
    return jax.shard_map(body, mesh=mesh, in_specs=in_specs, out_specs=out_specs, check_vma=False)
```

```python
import jax
import jax.numpy as jnp
from jax import lax
from jax.experimental import pallas as pl
from jax.experimental.pallas import tpu as pltpu
from jax.sharding import PartitionSpec as P

MESH = pl.DeviceIdType.MESH
F32 = jnp.float32
BF16 = jnp.bfloat16
NT = (((1,), (1,)), ((), ()))
TN = (((0,), (0,)), ((), ()))

NX, NY, NE = 4, 4, 8
CAP, ROWS, DEPTH, COLS, TOKS = 48, 192, 512, 1536, 128
GROUPS = 6
WIDE = COLS // GROUPS
LANES = 128
CHUNKS = COLS // LANES
PER_GROUP = WIDE // LANES
HOP = 3
STEPS = CHUNKS + HOP * (NE - 1)
FORWARD_AT, HGRAD_AT = 10, 16
WGRAD_AT = HGRAD_AT + NX


def kernel(
    ids_in, gates_in, hidden_in, weight_in, cot_in,
    mixed_ref, gate_ref, hgrad_ref, wgrad_ref,
    ids_ref, gates_ref, weight_ref, cot_ref,
    hid_all, hid_t, slot_all, cot_sel, parts, core_rx, core_sum, y_rx, z_own, z_tx, z_rx,
    tok, up_tx, up_rx, down_tx, down_rx, hg_tx, hg_rx, gate_tx, gate_sum, gate_xrx, gate_erx, gate_acc,
    in_sem, hid_sem, slot_z_sem, slot_y_sem, slot_c_sem, core_sem, y_sem, z_sem, up_sem, down_sem, hg_sem, gx_sem, ge_sem,
):
    dp = lax.axis_index("dp")
    ex = lax.axis_index("expert")
    mx = lax.axis_index("mp")
    core = dp % 2
    half = (dp // 2) % 2
    row = dp // 4

    def dp_of(y, h, c):
        return (y * 2 + h) * 2 + c

    def x_peer(d):
        return {"mp": (mx + d) % NX}

    def y_peer(d):
        return {"dp": dp_of((row + d) % NY, half, core)}

    def e_peer(d):
        return {"expert": (ex + d) % NE}

    core_peer = {"dp": dp_of(row, half, 1 - core)}
    half_peer = {"dp": dp_of(row, 1 - half, core)}

    def remote(src, dst, sems, index, peer):
        return pltpu.make_async_remote_copy(
            src_ref=src,
            dst_ref=dst,
            send_sem=sems.at[(0, *index)],
            recv_sem=sems.at[(1, *index)],
            device_id=peer,
            device_id_type=MESH,
        )

    barrier = pltpu.get_barrier_semaphore()
    peers = [x_peer(d) for d in range(1, NX)] + [y_peer(d) for d in range(1, NY)]
    peers += [e_peer(d) for d in range(1, NE)] + [core_peer, half_peer]
    for peer in peers:
        pl.semaphore_signal(barrier, inc=1, device_id=peer, device_id_type=MESH)

    def fetch(src, dst, index):
        return pltpu.make_async_copy(src, dst, in_sem.at[index])

    fetches = [
        fetch(ids_in, ids_ref, 0),
        fetch(gates_in, gates_ref, 1),
        fetch(hidden_in, hid_all.at[mx], 2),
        fetch(cot_in, cot_ref, 3),
        fetch(weight_in, weight_ref, 4),
    ]
    for copy in fetches:
        copy.start()

    fetches[2].wait()
    pl.semaphore_wait(barrier, len(peers))

    hid_copies = [
        remote(hid_all.at[mx], hid_all.at[mx], hid_sem, (d - 1,), x_peer(d)) for d in (1, 3, 2)
    ]
    for copy in hid_copies:
        copy.start()

    fetches[0].wait()
    fetches[1].wait()
    hit0 = (ids_ref[0:1, :] == ex).astype(F32)
    hit1 = (ids_ref[1:2, :] == ex).astype(F32)
    hits = hit0 + hit1
    gate_of = hit0 * gates_ref[0:1, :] + hit1 * gates_ref[1:2, :]
    earlier = lax.broadcasted_iota(jnp.int32, (TOKS, TOKS), 0) < lax.broadcasted_iota(
        jnp.int32, (TOKS, TOKS), 1
    )
    place = jnp.dot(
        jnp.broadcast_to(hits, (16, TOKS)).astype(BF16),
        earlier.astype(F32).astype(BF16),
        preferred_element_type=F32,
    )[0:1, :]
    slot = lax.broadcasted_iota(jnp.int32, (CAP, TOKS), 0).astype(F32)
    sel = jnp.where(slot == place, jnp.broadcast_to(hits, (CAP, TOKS)), 0.0)
    slot_gate = jnp.sum(sel * gate_of, axis=1, keepdims=True)
    sel16 = sel.astype(BF16)
    fetches[3].wait()
    picked = jnp.dot(sel16, cot_ref[...], preferred_element_type=F32)
    for g in range(GROUPS):
        cot_sel[g] = picked[:, g * WIDE : (g + 1) * WIDE]
    slot_all[dp] = (slot_gate * picked).astype(BF16)
    gate_acc[...] = jnp.zeros_like(gate_acc)

    def slot_y(side, block):
        return [
            remote(slot_all.at[block], slot_all.at[block], slot_y_sem, (side, d - 1), y_peer(d))
            for d in (1, 3, 2)
        ]

    def slot_core(index, block):
        return remote(slot_all.at[block], slot_all.at[block], slot_c_sem, (index,), core_peer)

    other_block = dp_of(row, 1 - half, core)
    slot_z = remote(slot_all.at[dp], slot_all.at[dp], slot_z_sem, (0,), half_peer)
    slot_z.start()
    own_y = slot_y(0, dp)
    for copy in own_y:
        copy.start()
    core_copies = [slot_core(0, dp)]
    core_copies[0].start()

    fetches[4].wait()

    def core_copy(block, g):
        return remote(
            parts.at[block, g, 1 - core], core_rx.at[block, g], core_sem, (block, g), core_peer
        )

    def row_copy(d, g):
        return remote(
            core_sum.at[(row + d) % NY, g], y_rx.at[g, d - 1], y_sem, (g, d - 1), y_peer(d)
        )

    to_z = []
    for copy, d in [(None, 0), *zip(hid_copies, (1, 3, 2))]:
        block = (mx - d + NX) % NX
        if copy is not None:
            copy.wait_recv()
        for g in range(GROUPS):
            product = jnp.dot(
                hid_all[block],
                weight_ref[:, g * WIDE : (g + 1) * WIDE],
                preferred_element_type=F32,
            ).astype(BF16)
            product = product.reshape(2, 2, CAP, WIDE)
            for c in range(2):
                parts[block, g, c] = product[:, c]
            core_copy(block, g).start()
        away = (block - row + NY) % NY
        for g in range(GROUPS):
            core_copy(block, g).wait_recv()
            core_sum[block, g] = (
                parts[block, g, core].astype(F32) + core_rx[block, g].astype(F32)
            ).astype(BF16)

            @pl.when(away > 0)
            def _():
                row_copy(away, g).start()


    for n, copy in enumerate(own_y):
        copy.wait_recv()
        d = (1, 3, 2)[n]
        onward = slot_core(1 + n, dp_of((row - d + NY) % NY, half, core))
        onward.start()
        core_copies.append(onward)
    hid_t[...] = hid_all[...].reshape(NX * ROWS, DEPTH).T
    other_y = slot_y(1, other_block)

    for g in range(GROUPS):
        for d in range(1, NY):
            row_copy(d, g).wait_recv()
        mine = core_sum[row, g].astype(F32)
        for d in range(1, NY):
            mine = mine + y_rx[g, d - 1].astype(F32)
        z_own[g] = mine
        z_tx[g] = z_own[g, 1 - half].astype(BF16)
        copy = remote(z_tx.at[g], z_rx.at[g], z_sem, (g,), half_peer)
        copy.start()
        to_z.append(copy)
        if g == GROUPS // 2:
            slot_z.wait_recv()
            for copy in other_y:
                copy.start()
            onward = slot_core(4, other_block)
            onward.start()
            core_copies.append(onward)
    onwards = [
        slot_core(5 + n, dp_of((row - d + NY) % NY, 1 - half, core))
        for n, d in enumerate((1, 3, 2))
    ]
    core_copies += onwards

    sel_t = sel.T.astype(BF16)

    def take_group(g):
        remote(z_tx.at[g], z_rx.at[g], z_sem, (g,), half_peer).wait_recv()
        out = (z_own[g, half] + z_rx[g].astype(F32)).astype(BF16).astype(F32)
        gate_acc[...] += jnp.sum(out * cot_sel[g], axis=1, keepdims=True)
        weighted = jnp.dot(
            sel_t, (slot_gate * out).astype(BF16), preferred_element_type=F32
        ).astype(BF16)
        for n in range(PER_GROUP):
            tok[g * PER_GROUP + n] = weighted[:, n * LANES : (n + 1) * LANES]

    up_peer, down_peer = e_peer(1), e_peer(NE - 1)

    def up_copy(q):
        return remote(up_tx.at[q], up_rx.at[q], up_sem, (q,), up_peer)

    def down_copy(q):
        return remote(down_tx.at[q], down_rx.at[q], down_sem, (q,), down_peer)

    gate_x = [remote(gate_tx, gate_xrx.at[d - 1], gx_sem, (d - 1,), x_peer(d)) for d in (2, 1, 3)]
    gate_e = [
        remote(gate_sum, gate_erx.at[d - 1], ge_sem, (d - 1,), e_peer(d)) for d in range(1, NE)
    ]
    hg_copies = [
        remote(hg_tx.at[(mx + d) % NX], hg_rx.at[d - 1], hg_sem, (d - 1,), x_peer(d))
        for d in (2, 1, 3)
    ]

    def step(s, carry):
        @pl.when(jnp.logical_and(s % PER_GROUP == 0, s < CHUNKS))
        def _():
            take_group(s // PER_GROUP)

        @pl.when(s == CHUNKS - 1)
        def _():
            per_token = jnp.sum(sel * gate_acc[:, 0:1], axis=0, keepdims=True)
            gate_tx[...] = jnp.zeros_like(gate_tx)
            gate_tx[0:1, :] = per_token * hit0
            gate_tx[1:2, :] = per_token * hit1
            for copy in gate_x:
                copy.start()

        @pl.when(s == CHUNKS + 3)
        def _():
            for copy in gate_x:
                copy.wait_recv()
            gate_sum[...] = gate_tx[...] + gate_xrx[0] + gate_xrx[1] + gate_xrx[2]
            for copy in gate_e:
                copy.start()

        q = s - HOP * ex

        @pl.when(jnp.logical_and(q >= 0, q < CHUNKS))
        def _():
            @pl.when(ex == 0)
            def _():
                up_tx[q] = tok[q]

            @pl.when(ex > 0)
            def _():
                up_copy(q).wait_recv()
                up_tx[q] = (tok[q].astype(F32) + up_rx[q].astype(F32)).astype(BF16)

            @pl.when(ex < NE - 1)
            def _():
                up_copy(q).start()

        r = s - HOP * (NE - 1 - ex)

        @pl.when(jnp.logical_and(r >= 0, r < CHUNKS))
        def _():
            @pl.when(ex == NE - 1)
            def _():
                down_tx[r] = tok[r]

            @pl.when(ex < NE - 1)
            def _():
                down_copy(r).wait_recv()
                down_tx[r] = (tok[r].astype(F32) + down_rx[r].astype(F32)).astype(BF16)

            @pl.when(ex > 0)
            def _():
                down_copy(r).start()

        @pl.when(s == FORWARD_AT)
        def _():
            for copy, onward in zip(other_y, onwards):
                copy.wait_recv()
                onward.start()

        @pl.when(s == HGRAD_AT)
        def _():
            for copy in core_copies:
                copy.wait_recv()

        for n, d in enumerate((2, 1, 3, 0)):

            @pl.when(s == HGRAD_AT + n)
            def _():
                block = (mx + d) % NX
                slots = slot_all[pl.ds(block * 4, 4)].reshape(ROWS, COLS)
                hg_tx[block] = lax.dot_general(
                    slots, weight_ref[...], NT, preferred_element_type=F32
                ).astype(BF16)
                if d:
                    hg_copies[n].start()

        for g in range(GROUPS):

            @pl.when(s == WGRAD_AT + g)
            def _():
                columns = slice(g * WIDE, (g + 1) * WIDE)
                wgrad_ref[:, columns] = jnp.dot(
                    hid_t[...],
                    slot_all[:, :, columns].reshape(NX * ROWS, WIDE),
                    preferred_element_type=F32,
                ).astype(BF16)

        return carry

    lax.fori_loop(0, STEPS, step, 0)

    for q in range(CHUNKS):
        columns = slice(q * LANES, (q + 1) * LANES)

        @pl.when(ex < NE - 1)
        def _():
            mixed_ref[:, columns] = (up_tx[q].astype(F32) + down_rx[q].astype(F32)).astype(BF16)

        @pl.when(ex == NE - 1)
        def _():
            mixed_ref[:, columns] = up_tx[q]

    for copy in hg_copies:
        copy.wait_recv()
    total = hg_tx[mx].astype(F32)
    for d in range(1, NX):
        total = total + hg_rx[d - 1].astype(F32)
    hgrad_ref[...] = total.astype(BF16)

    for copy in gate_e:
        copy.wait_recv()
    gates = gate_sum[...]
    for d in range(1, NE):
        gates = gates + gate_erx[d - 1]
    gate_ref[...] = gates[0:2, :]

    for copy in [*hid_copies, slot_z, *own_y, *other_y, *core_copies, *to_z]:
        copy.wait_send()
    for g in range(GROUPS):
        for block in range(NY):
            core_copy(block, g).wait_send()
        for d in range(1, NY):
            row_copy(d, g).wait_send()
    for copy in [*hg_copies, *gate_x, *gate_e]:
        copy.wait_send()

    def drain(q, carry):
        @pl.when(ex < NE - 1)
        def _():
            up_copy(q).wait_send()

        @pl.when(ex > 0)
        def _():
            down_copy(q).wait_send()

        return carry

    lax.fori_loop(0, CHUNKS, drain, 0)


def body(expert_ids, gate_weights, hidden, down_weight, cotangent):
    vmem = pl.BlockSpec(memory_space=pltpu.VMEM)
    hbm = pl.BlockSpec(memory_space=pltpu.HBM)
    dma = pltpu.SemaphoreType.DMA
    shapes = (
        jax.ShapeDtypeStruct((TOKS, COLS), BF16),
        jax.ShapeDtypeStruct((2, TOKS), F32),
        jax.ShapeDtypeStruct((ROWS, DEPTH), BF16),
        jax.ShapeDtypeStruct((DEPTH, COLS), BF16),
    )
    operands = (expert_ids.T, gate_weights.T, hidden[0], down_weight[0], cotangent)
    operands = [pltpu.with_memory_space_constraint(each, pltpu.HBM) for each in operands]
    mixed, gates, hgrad, wgrad = pl.pallas_call(
        kernel,
        name="layer",
        out_shape=shapes,
        in_specs=[hbm] * 5,
        out_specs=(vmem,) * 4,
        scratch_shapes=[
            pltpu.VMEM((2, TOKS), jnp.int32),
            pltpu.VMEM((2, TOKS), F32),
            pltpu.VMEM((DEPTH, COLS), BF16),
            pltpu.VMEM((TOKS, COLS), BF16),
            pltpu.VMEM((NX, ROWS, DEPTH), BF16),
            pltpu.VMEM((DEPTH, NX * ROWS), BF16),
            pltpu.VMEM((16, CAP, COLS), BF16),
            pltpu.VMEM((GROUPS, CAP, WIDE), F32),
            pltpu.VMEM((NY, GROUPS, 2, 2, CAP, WIDE), BF16),
            pltpu.VMEM((NY, GROUPS, 2, CAP, WIDE), BF16),
            pltpu.VMEM((NY, GROUPS, 2, CAP, WIDE), BF16),
            pltpu.VMEM((GROUPS, NY - 1, 2, CAP, WIDE), BF16),
            pltpu.VMEM((GROUPS, 2, CAP, WIDE), F32),
            pltpu.VMEM((GROUPS, CAP, WIDE), BF16),
            pltpu.VMEM((GROUPS, CAP, WIDE), BF16),
            pltpu.VMEM((CHUNKS, TOKS, LANES), BF16),
            pltpu.VMEM((CHUNKS, TOKS, LANES), BF16),
            pltpu.VMEM((CHUNKS, TOKS, LANES), BF16),
            pltpu.VMEM((CHUNKS, TOKS, LANES), BF16),
            pltpu.VMEM((CHUNKS, TOKS, LANES), BF16),
            pltpu.VMEM((NX, ROWS, DEPTH), BF16),
            pltpu.VMEM((NX - 1, ROWS, DEPTH), BF16),
            pltpu.VMEM((8, TOKS), F32),
            pltpu.VMEM((8, TOKS), F32),
            pltpu.VMEM((NX - 1, 8, TOKS), F32),
            pltpu.VMEM((NE - 1, 8, TOKS), F32),
            pltpu.VMEM((CAP, TOKS), F32),
            dma((5,)),
            dma((2, NX - 1)),
            dma((2, 1)),
            dma((2, 2, NY - 1)),
            dma((2, 8)),
            dma((2, NY, GROUPS)),
            dma((2, GROUPS, NY - 1)),
            dma((2, GROUPS)),
            dma((2, CHUNKS)),
            dma((2, CHUNKS)),
            dma((2, NX - 1)),
            dma((2, NX - 1)),
            dma((2, NE - 1)),
        ],
        compiler_params=pltpu.CompilerParams(
            collective_id=0, has_side_effects=True, vmem_limit_bytes=50 * 2**20
        ),
    )(*operands)
    return mixed, gates.T, hgrad[None], wgrad[None]


def solution(mesh):
    in_specs = (
        P("dp", None),
        P("dp", None),
        P("expert", "mp", "dp"),
        P("expert", "dp", "mp"),
        P("dp", "mp"),
    )
    out_specs = (P("dp", "mp"), P("dp", None), P("expert", "mp", "dp"), P("expert", "dp", "mp"))
    return jax.shard_map(body, mesh=mesh, in_specs=in_specs, out_specs=out_specs, check_vma=False)
```

```python
import jax
import jax.numpy as jnp
from jax import lax
from jax.experimental import pallas as pl
from jax.experimental.pallas import tpu as pltpu
from jax.sharding import PartitionSpec as P

MESH = pl.DeviceIdType.MESH
F32 = jnp.float32
BF16 = jnp.bfloat16
NT = (((1,), (1,)), ((), ()))
TN = (((0,), (0,)), ((), ()))

NX, NY, NE = 4, 4, 8
CAP, ROWS, DEPTH, COLS, TOKS = 48, 192, 512, 1536, 128
GROUPS = 6
WIDE = COLS // GROUPS
LANES = 128
CHUNKS = COLS // LANES
PER_GROUP = WIDE // LANES
HOP = 5
STEPS = CHUNKS + HOP * (NE - 1)
FORWARD_AT, HGRAD_AT = 10, 16
WGRAD_AT = HGRAD_AT + NX


def kernel(
    ids_in, gates_in, hidden_in, weight_in, cot_in,
    mixed_ref, gate_ref, hgrad_ref, wgrad_ref,
    ids_ref, gates_ref, weight_ref, cot_ref,
    hid_all, hid_t, slot_all, cot_sel, parts, core_rx, core_sum, y_rx, z_own, z_tx, z_rx,
    tok, up_tx, up_rx, down_tx, down_rx, hg_tx, hg_rx, gate_tx, gate_sum, gate_xrx, gate_erx, gate_acc,
    in_sem, hid_sem, slot_z_sem, slot_y_sem, slot_c_sem, core_sem, y_sem, z_sem, up_sem, down_sem, hg_sem, gx_sem, ge_sem,
):
    dp = lax.axis_index("dp")
    ex = lax.axis_index("expert")
    mx = lax.axis_index("mp")
    core = dp % 2
    half = (dp // 2) % 2
    row = dp // 4

    def dp_of(y, h, c):
        return (y * 2 + h) * 2 + c

    def x_peer(d):
        return {"mp": (mx + d) % NX}

    def y_peer(d):
        return {"dp": dp_of((row + d) % NY, half, core)}

    def e_peer(d):
        return {"expert": (ex + d) % NE}

    core_peer = {"dp": dp_of(row, half, 1 - core)}
    half_peer = {"dp": dp_of(row, 1 - half, core)}

    def remote(src, dst, sems, index, peer):
        return pltpu.make_async_remote_copy(
            src_ref=src,
            dst_ref=dst,
            send_sem=sems.at[(0, *index)],
            recv_sem=sems.at[(1, *index)],
            device_id=peer,
            device_id_type=MESH,
        )

    barrier = pltpu.get_barrier_semaphore()
    peers = [x_peer(d) for d in range(1, NX)] + [y_peer(d) for d in range(1, NY)]
    peers += [e_peer(d) for d in range(1, NE)] + [core_peer, half_peer]
    for peer in peers:
        pl.semaphore_signal(barrier, inc=1, device_id=peer, device_id_type=MESH)

    def fetch(src, dst, index):
        return pltpu.make_async_copy(src, dst, in_sem.at[index])

    fetches = [
        fetch(ids_in, ids_ref, 0),
        fetch(gates_in, gates_ref, 1),
        fetch(hidden_in, hid_all.at[mx], 2),
        fetch(cot_in, cot_ref, 3),
        fetch(weight_in, weight_ref, 4),
    ]
    for copy in fetches:
        copy.start()

    fetches[2].wait()
    pl.semaphore_wait(barrier, len(peers))

    hid_copies = [
        remote(hid_all.at[mx], hid_all.at[mx], hid_sem, (d - 1,), x_peer(d)) for d in (1, 3, 2)
    ]
    for copy in hid_copies:
        copy.start()

    fetches[0].wait()
    fetches[1].wait()
    hit0 = (ids_ref[0:1, :] == ex).astype(F32)
    hit1 = (ids_ref[1:2, :] == ex).astype(F32)
    hits = hit0 + hit1
    gate_of = hit0 * gates_ref[0:1, :] + hit1 * gates_ref[1:2, :]
    earlier = lax.broadcasted_iota(jnp.int32, (TOKS, TOKS), 0) < lax.broadcasted_iota(
        jnp.int32, (TOKS, TOKS), 1
    )
    place = jnp.dot(
        jnp.broadcast_to(hits, (16, TOKS)).astype(BF16),
        earlier.astype(F32).astype(BF16),
        preferred_element_type=F32,
    )[0:1, :]
    slot = lax.broadcasted_iota(jnp.int32, (CAP, TOKS), 0).astype(F32)
    sel = jnp.where(slot == place, jnp.broadcast_to(hits, (CAP, TOKS)), 0.0)
    slot_gate = jnp.sum(sel * gate_of, axis=1, keepdims=True)
    sel16 = sel.astype(BF16)
    fetches[3].wait()
    picked = jnp.dot(sel16, cot_ref[...], preferred_element_type=F32)
    for g in range(GROUPS):
        cot_sel[g] = picked[:, g * WIDE : (g + 1) * WIDE]
    slot_all[dp] = (slot_gate * picked).astype(BF16)
    gate_acc[...] = jnp.zeros_like(gate_acc)

    def slot_y(side, block):
        return [
            remote(slot_all.at[block], slot_all.at[block], slot_y_sem, (side, d - 1), y_peer(d))
            for d in (1, 3, 2)
        ]

    def slot_core(index, block):
        return remote(slot_all.at[block], slot_all.at[block], slot_c_sem, (index,), core_peer)

    other_block = dp_of(row, 1 - half, core)
    slot_z = remote(slot_all.at[dp], slot_all.at[dp], slot_z_sem, (0,), half_peer)
    slot_z.start()
    own_y = slot_y(0, dp)
    for copy in own_y:
        copy.start()
    core_copies = [slot_core(0, dp)]
    core_copies[0].start()

    fetches[4].wait()

    def core_copy(g):
        return remote(parts.at[g, 1 - core], core_rx.at[g], core_sem, (g,), core_peer)

    def row_copy(d, g):
        return remote(
            core_sum.at[g, (row + d) % NY], y_rx.at[g, d - 1], y_sem, (g, d - 1), y_peer(d)
        )

    to_z = []
    for copy in hid_copies:
        copy.wait_recv()
    rows_all = hid_all[...].reshape(NX * ROWS, DEPTH)
    for g in range(GROUPS + 2):
        if g < GROUPS:
            product = jnp.dot(
                rows_all, weight_ref[:, g * WIDE : (g + 1) * WIDE], preferred_element_type=F32
            ).astype(BF16)
            product = product.reshape(NY, 2, 2, CAP, WIDE)
            for c in range(2):
                parts[g, c] = product[:, :, c]
            core_copy(g).start()
        if g >= 2:
            n = g - 2
            core_copy(n).wait_recv()
            core_sum[n] = (parts[n, core].astype(F32) + core_rx[n].astype(F32)).astype(BF16)
            for d in (2, 1, 3):
                row_copy(d, n).start()


    for n, copy in enumerate(own_y):
        copy.wait_recv()
        d = (1, 3, 2)[n]
        onward = slot_core(1 + n, dp_of((row - d + NY) % NY, half, core))
        onward.start()
        core_copies.append(onward)
    hid_t[...] = hid_all[...].reshape(NX * ROWS, DEPTH).T
    other_y = slot_y(1, other_block)

    for g in range(GROUPS):
        for d in range(1, NY):
            row_copy(d, g).wait_recv()
        mine = core_sum[g, row].astype(F32)
        for d in range(1, NY):
            mine = mine + y_rx[g, d - 1].astype(F32)
        z_own[g] = mine
        z_tx[g] = z_own[g, 1 - half].astype(BF16)
        copy = remote(z_tx.at[g], z_rx.at[g], z_sem, (g,), half_peer)
        copy.start()
        to_z.append(copy)
        if g == GROUPS // 2:
            slot_z.wait_recv()
            for copy in other_y:
                copy.start()
            onward = slot_core(4, other_block)
            onward.start()
            core_copies.append(onward)
    onwards = [
        slot_core(5 + n, dp_of((row - d + NY) % NY, 1 - half, core))
        for n, d in enumerate((1, 3, 2))
    ]
    core_copies += onwards

    sel_t = sel.T.astype(BF16)

    def take_group(g):
        remote(z_tx.at[g], z_rx.at[g], z_sem, (g,), half_peer).wait_recv()
        out = (z_own[g, half] + z_rx[g].astype(F32)).astype(BF16).astype(F32)
        gate_acc[...] += jnp.sum(out * cot_sel[g], axis=1, keepdims=True)
        weighted = jnp.dot(
            sel_t, (slot_gate * out).astype(BF16), preferred_element_type=F32
        ).astype(BF16)
        for n in range(PER_GROUP):
            tok[g * PER_GROUP + n] = weighted[:, n * LANES : (n + 1) * LANES]

    up_peer, down_peer = e_peer(1), e_peer(NE - 1)

    def up_copy(q):
        return remote(up_tx.at[q], up_rx.at[q], up_sem, (q,), up_peer)

    def down_copy(q):
        return remote(down_tx.at[q], down_rx.at[q], down_sem, (q,), down_peer)

    gate_x = [remote(gate_tx, gate_xrx.at[d - 1], gx_sem, (d - 1,), x_peer(d)) for d in (2, 1, 3)]
    gate_e = [
        remote(gate_sum, gate_erx.at[d - 1], ge_sem, (d - 1,), e_peer(d)) for d in range(1, NE)
    ]
    hg_copies = [
        remote(hg_tx.at[(mx + d) % NX], hg_rx.at[d - 1], hg_sem, (d - 1,), x_peer(d))
        for d in (2, 1, 3)
    ]

    def step(s, carry):
        @pl.when(jnp.logical_and(s % PER_GROUP == 0, s < CHUNKS))
        def _():
            take_group(s // PER_GROUP)

        @pl.when(s == CHUNKS - 1)
        def _():
            per_token = jnp.sum(sel * gate_acc[:, 0:1], axis=0, keepdims=True)
            gate_tx[...] = jnp.zeros_like(gate_tx)
            gate_tx[0:1, :] = per_token * hit0
            gate_tx[1:2, :] = per_token * hit1
            for copy in gate_x:
                copy.start()

        @pl.when(s == CHUNKS + 3)
        def _():
            for copy in gate_x:
                copy.wait_recv()
            gate_sum[...] = gate_tx[...] + gate_xrx[0] + gate_xrx[1] + gate_xrx[2]
            for copy in gate_e:
                copy.start()

        q = s - HOP * ex

        @pl.when(jnp.logical_and(q >= 0, q < CHUNKS))
        def _():
            @pl.when(ex == 0)
            def _():
                up_tx[q] = tok[q]

            @pl.when(ex > 0)
            def _():
                up_copy(q).wait_recv()
                up_tx[q] = (tok[q].astype(F32) + up_rx[q].astype(F32)).astype(BF16)

            @pl.when(ex < NE - 1)
            def _():
                up_copy(q).start()

        r = s - HOP * (NE - 1 - ex)

        @pl.when(jnp.logical_and(r >= 0, r < CHUNKS))
        def _():
            @pl.when(ex == NE - 1)
            def _():
                down_tx[r] = tok[r]

            @pl.when(ex < NE - 1)
            def _():
                down_copy(r).wait_recv()
                down_tx[r] = (tok[r].astype(F32) + down_rx[r].astype(F32)).astype(BF16)

            @pl.when(ex > 0)
            def _():
                down_copy(r).start()

        @pl.when(s == FORWARD_AT)
        def _():
            for copy, onward in zip(other_y, onwards):
                copy.wait_recv()
                onward.start()

        @pl.when(s == HGRAD_AT)
        def _():
            for copy in core_copies:
                copy.wait_recv()

        for n, d in enumerate((2, 1, 3, 0)):

            @pl.when(s == HGRAD_AT + n)
            def _():
                block = (mx + d) % NX
                slots = slot_all[pl.ds(block * 4, 4)].reshape(ROWS, COLS)
                hg_tx[block] = lax.dot_general(
                    slots, weight_ref[...], NT, preferred_element_type=F32
                ).astype(BF16)
                if d:
                    hg_copies[n].start()

        for g in range(GROUPS):

            @pl.when(s == WGRAD_AT + g)
            def _():
                columns = slice(g * WIDE, (g + 1) * WIDE)
                wgrad_ref[:, columns] = jnp.dot(
                    hid_t[...],
                    slot_all[:, :, columns].reshape(NX * ROWS, WIDE),
                    preferred_element_type=F32,
                ).astype(BF16)

        return carry

    lax.fori_loop(0, STEPS, step, 0)

    for q in range(CHUNKS):
        columns = slice(q * LANES, (q + 1) * LANES)

        @pl.when(ex < NE - 1)
        def _():
            mixed_ref[:, columns] = (up_tx[q].astype(F32) + down_rx[q].astype(F32)).astype(BF16)

        @pl.when(ex == NE - 1)
        def _():
            mixed_ref[:, columns] = up_tx[q]

    for copy in hg_copies:
        copy.wait_recv()
    total = hg_tx[mx].astype(F32)
    for d in range(1, NX):
        total = total + hg_rx[d - 1].astype(F32)
    hgrad_ref[...] = total.astype(BF16)

    for copy in gate_e:
        copy.wait_recv()
    gates = gate_sum[...]
    for d in range(1, NE):
        gates = gates + gate_erx[d - 1]
    gate_ref[...] = gates[0:2, :]

    for copy in [*hid_copies, slot_z, *own_y, *other_y, *core_copies, *to_z]:
        copy.wait_send()
    for g in range(GROUPS):
        core_copy(g).wait_send()
        for d in range(1, NY):
            row_copy(d, g).wait_send()
    for copy in [*hg_copies, *gate_x, *gate_e]:
        copy.wait_send()

    def drain(q, carry):
        @pl.when(ex < NE - 1)
        def _():
            up_copy(q).wait_send()

        @pl.when(ex > 0)
        def _():
            down_copy(q).wait_send()

        return carry

    lax.fori_loop(0, CHUNKS, drain, 0)


def write_out(*refs):
    count = (len(refs) - 1) // 2
    copies = [
        pltpu.make_async_copy(refs[n], refs[count + n], refs[-1].at[n]) for n in range(count)
    ]
    for copy in copies:
        copy.start()
    for copy in copies:
        copy.wait()


def body(expert_ids, gate_weights, hidden, down_weight, cotangent):
    vmem = pl.BlockSpec(memory_space=pltpu.VMEM)
    hbm = pl.BlockSpec(memory_space=pltpu.HBM)
    dma = pltpu.SemaphoreType.DMA
    shapes = (
        jax.ShapeDtypeStruct((TOKS, COLS), BF16),
        jax.ShapeDtypeStruct((2, TOKS), F32),
        jax.ShapeDtypeStruct((ROWS, DEPTH), BF16),
        jax.ShapeDtypeStruct((DEPTH, COLS), BF16),
    )
    operands = (expert_ids.T, gate_weights.T, hidden[0], down_weight[0], cotangent)
    operands = [pltpu.with_memory_space_constraint(each, pltpu.HBM) for each in operands]
    results = pl.pallas_call(
        kernel,
        name="layer",
        out_shape=shapes,
        in_specs=[hbm] * 5,
        out_specs=(vmem,) * 4,
        scratch_shapes=[
            pltpu.VMEM((2, TOKS), jnp.int32),
            pltpu.VMEM((2, TOKS), F32),
            pltpu.VMEM((DEPTH, COLS), BF16),
            pltpu.VMEM((TOKS, COLS), BF16),
            pltpu.VMEM((NX, ROWS, DEPTH), BF16),
            pltpu.VMEM((DEPTH, NX * ROWS), BF16),
            pltpu.VMEM((16, CAP, COLS), BF16),
            pltpu.VMEM((GROUPS, CAP, WIDE), F32),
            pltpu.VMEM((GROUPS, 2, NY, 2, CAP, WIDE), BF16),
            pltpu.VMEM((GROUPS, NY, 2, CAP, WIDE), BF16),
            pltpu.VMEM((GROUPS, NY, 2, CAP, WIDE), BF16),
            pltpu.VMEM((GROUPS, NY - 1, 2, CAP, WIDE), BF16),
            pltpu.VMEM((GROUPS, 2, CAP, WIDE), F32),
            pltpu.VMEM((GROUPS, CAP, WIDE), BF16),
            pltpu.VMEM((GROUPS, CAP, WIDE), BF16),
            pltpu.VMEM((CHUNKS, TOKS, LANES), BF16),
            pltpu.VMEM((CHUNKS, TOKS, LANES), BF16),
            pltpu.VMEM((CHUNKS, TOKS, LANES), BF16),
            pltpu.VMEM((CHUNKS, TOKS, LANES), BF16),
            pltpu.VMEM((CHUNKS, TOKS, LANES), BF16),
            pltpu.VMEM((NX, ROWS, DEPTH), BF16),
            pltpu.VMEM((NX - 1, ROWS, DEPTH), BF16),
            pltpu.VMEM((8, TOKS), F32),
            pltpu.VMEM((8, TOKS), F32),
            pltpu.VMEM((NX - 1, 8, TOKS), F32),
            pltpu.VMEM((NE - 1, 8, TOKS), F32),
            pltpu.VMEM((CAP, TOKS), F32),
            dma((5,)),
            dma((2, NX - 1)),
            dma((2, 1)),
            dma((2, 2, NY - 1)),
            dma((2, 8)),
            dma((2, GROUPS)),
            dma((2, GROUPS, NY - 1)),
            dma((2, GROUPS)),
            dma((2, CHUNKS)),
            dma((2, CHUNKS)),
            dma((2, NX - 1)),
            dma((2, NX - 1)),
            dma((2, NE - 1)),
        ],
        compiler_params=pltpu.CompilerParams(
            collective_id=0, has_side_effects=True, vmem_limit_bytes=50 * 2**20
        ),
    )(*operands)
    results = [pltpu.with_memory_space_constraint(each, pltpu.VMEM) for each in results]
    mixed, gates, hgrad, wgrad = pl.pallas_call(
        write_out,
        name="write_out",
        out_shape=shapes,
        in_specs=[vmem] * 4,
        out_specs=(hbm,) * 4,
        scratch_shapes=[dma((4,))],
    )(*results)
    return mixed, gates.T, hgrad[None], wgrad[None]


def solution(mesh):
    in_specs = (
        P("dp", None),
        P("dp", None),
        P("expert", "mp", "dp"),
        P("expert", "dp", "mp"),
        P("dp", "mp"),
    )
    out_specs = (P("dp", "mp"), P("dp", None), P("expert", "mp", "dp"), P("expert", "dp", "mp"))
    return jax.shard_map(body, mesh=mesh, in_specs=in_specs, out_specs=out_specs, check_vma=False)
```

```python
import jax
import jax.numpy as jnp
from jax import lax
from jax.experimental import pallas as pl
from jax.experimental.pallas import tpu as pltpu
from jax.sharding import PartitionSpec as P

MESH = pl.DeviceIdType.MESH
F32 = jnp.float32
BF16 = jnp.bfloat16
NT = (((1,), (1,)), ((), ()))
TN = (((0,), (0,)), ((), ()))

NX, NY, NE = 4, 4, 8
CAP, ROWS, DEPTH, COLS, TOKS = 48, 192, 512, 1536, 128
HALF_ROWS = ROWS // 2
GROUPS = 6
WIDE = COLS // GROUPS
LANES = 128
CHUNKS = COLS // LANES
PER_GROUP = WIDE // LANES
HOP = 5
STEPS = CHUNKS + HOP * (NE - 1)
FORWARD_AT, HGRAD_AT = 10, 16
WGRAD_AT = HGRAD_AT + NX


def kernel(
    ids_in, gates_in, hidden_in, weight_in, cot_in,
    mixed_ref, gate_ref, hgrad_ref, wgrad_ref,
    ids_ref, gates_ref, weight_ref, cot_ref,
    hid_all, hid_t, slot_all, cot_sel, parts, core_rx, core_sum, y_rx, z_own, z_tx, z_rx,
    tok, up_tx, up_rx, down_tx, down_rx, hg_tx, hg_rx, gate_tx, gate_sum, gate_xrx, gate_erx, gate_acc,
    in_sem, hid_sem, slot_z_sem, slot_y_sem, slot_c_sem, core_sem, y_sem, z_sem, up_sem, down_sem, hg_sem, gx_sem, ge_sem,
):
    dp = lax.axis_index("dp")
    ex = lax.axis_index("expert")
    mx = lax.axis_index("mp")
    core = dp % 2
    half = (dp // 2) % 2
    row = dp // 4

    def dp_of(y, h, c):
        return (y * 2 + h) * 2 + c

    def x_peer(d):
        return {"mp": (mx + d) % NX}

    def y_peer(d):
        return {"dp": dp_of((row + d) % NY, half, core)}

    def e_peer(d):
        return {"expert": (ex + d) % NE}

    core_peer = {"dp": dp_of(row, half, 1 - core)}
    half_peer = {"dp": dp_of(row, 1 - half, core)}

    def remote(src, dst, sems, index, peer):
        return pltpu.make_async_remote_copy(
            src_ref=src,
            dst_ref=dst,
            send_sem=sems.at[(0, *index)],
            recv_sem=sems.at[(1, *index)],
            device_id=peer,
            device_id_type=MESH,
        )

    barrier = pltpu.get_barrier_semaphore()
    peers = [x_peer(d) for d in range(1, NX)] + [y_peer(d) for d in range(1, NY)]
    peers += [e_peer(d) for d in range(1, NE)] + [core_peer, half_peer]
    for peer in peers:
        pl.semaphore_signal(barrier, inc=1, device_id=peer, device_id_type=MESH)

    def fetch(src, dst, index):
        return pltpu.make_async_copy(src, dst, in_sem.at[index])

    fetches = [
        fetch(ids_in, ids_ref, 0),
        fetch(gates_in, gates_ref, 1),
        fetch(hidden_in, hid_all.at[mx], 2),
        fetch(cot_in, cot_ref, 3),
        fetch(weight_in, weight_ref, 4),
    ]
    for copy in fetches:
        copy.start()

    fetches[2].wait()
    pl.semaphore_wait(barrier, len(peers))

    def hid_copy(index, block, part, d):
        ref = hid_all.at[block, pl.ds(part * HALF_ROWS, HALF_ROWS)]
        return remote(ref, ref, hid_sem, (index,), x_peer(d))

    right, left = 1, NX - 1
    hid_copies = [
        hid_copy(0, mx, 0, right),
        hid_copy(1, mx, 1, left),
        hid_copy(2, mx, 1, right),
        hid_copy(3, mx, 0, left),
    ]
    hid_onward = [
        hid_copy(4, (mx + left) % NX, 0, right),
        hid_copy(5, (mx + right) % NX, 1, left),
    ]
    for copy in hid_copies:
        copy.start()

    fetches[0].wait()
    fetches[1].wait()
    hit0 = (ids_ref[0:1, :] == ex).astype(F32)
    hit1 = (ids_ref[1:2, :] == ex).astype(F32)
    hits = hit0 + hit1
    gate_of = hit0 * gates_ref[0:1, :] + hit1 * gates_ref[1:2, :]
    earlier = lax.broadcasted_iota(jnp.int32, (TOKS, TOKS), 0) < lax.broadcasted_iota(
        jnp.int32, (TOKS, TOKS), 1
    )
    place = jnp.dot(
        jnp.broadcast_to(hits, (16, TOKS)).astype(BF16),
        earlier.astype(F32).astype(BF16),
        preferred_element_type=F32,
    )[0:1, :]
    slot = lax.broadcasted_iota(jnp.int32, (CAP, TOKS), 0).astype(F32)
    sel = jnp.where(slot == place, jnp.broadcast_to(hits, (CAP, TOKS)), 0.0)
    slot_gate = jnp.sum(sel * gate_of, axis=1, keepdims=True)
    sel16 = sel.astype(BF16)
    fetches[3].wait()
    picked = jnp.dot(sel16, cot_ref[...], preferred_element_type=F32)
    for g in range(GROUPS):
        cot_sel[g] = picked[:, g * WIDE : (g + 1) * WIDE]
    slot_all[dp] = (slot_gate * picked).astype(BF16)
    gate_acc[...] = jnp.zeros_like(gate_acc)

    def slot_y(side, block):
        return [
            remote(slot_all.at[block], slot_all.at[block], slot_y_sem, (side, d - 1), y_peer(d))
            for d in (1, 3, 2)
        ]

    def slot_core(index, block):
        return remote(slot_all.at[block], slot_all.at[block], slot_c_sem, (index,), core_peer)

    other_block = dp_of(row, 1 - half, core)
    slot_z = remote(slot_all.at[dp], slot_all.at[dp], slot_z_sem, (0,), half_peer)
    slot_z.start()
    own_y = slot_y(0, dp)
    for copy in own_y:
        copy.start()
    core_copies = [slot_core(0, dp)]
    core_copies[0].start()
    for copy, onward in zip(hid_copies, hid_onward):
        copy.wait_recv()
        onward.start()

    fetches[4].wait()

    def core_copy(g):
        return remote(parts.at[g, 1 - core], core_rx.at[g], core_sem, (g,), core_peer)

    def row_copy(d, g):
        return remote(
            core_sum.at[g, (row + d) % NY], y_rx.at[g, d - 1], y_sem, (g, d - 1), y_peer(d)
        )

    to_z = []
    for copy in [*hid_copies[2:], *hid_onward]:
        copy.wait_recv()
    rows_all = hid_all[...].reshape(NX * ROWS, DEPTH)
    for g in range(GROUPS + 2):
        if g < GROUPS:
            product = jnp.dot(
                rows_all, weight_ref[:, g * WIDE : (g + 1) * WIDE], preferred_element_type=F32
            ).astype(BF16)
            product = product.reshape(NY, 2, 2, CAP, WIDE)
            for c in range(2):
                parts[g, c] = product[:, :, c]
            core_copy(g).start()
        if g >= 2:
            n = g - 2
            core_copy(n).wait_recv()
            core_sum[n] = (parts[n, core].astype(F32) + core_rx[n].astype(F32)).astype(BF16)
            for d in (1, 3, 2):
                row_copy(d, n).start()


    for n, copy in enumerate(own_y):
        copy.wait_recv()
        d = (1, 3, 2)[n]
        onward = slot_core(1 + n, dp_of((row - d + NY) % NY, half, core))
        onward.start()
        core_copies.append(onward)
    hid_t[...] = hid_all[...].reshape(NX * ROWS, DEPTH).T
    other_y = slot_y(1, other_block)

    for g in range(GROUPS):
        for d in range(1, NY):
            row_copy(d, g).wait_recv()
        mine = core_sum[g, row].astype(F32)
        for d in range(1, NY):
            mine = mine + y_rx[g, d - 1].astype(F32)
        z_own[g] = mine
        z_tx[g] = z_own[g, 1 - half].astype(BF16)
        copy = remote(z_tx.at[g], z_rx.at[g], z_sem, (g,), half_peer)
        copy.start()
        to_z.append(copy)
        if g == GROUPS // 2:
            slot_z.wait_recv()
            for copy in other_y:
                copy.start()
            onward = slot_core(4, other_block)
            onward.start()
            core_copies.append(onward)
    onwards = [
        slot_core(5 + n, dp_of((row - d + NY) % NY, 1 - half, core))
        for n, d in enumerate((1, 3, 2))
    ]
    core_copies += onwards

    sel_t = sel.T.astype(BF16)

    def take_group(g):
        remote(z_tx.at[g], z_rx.at[g], z_sem, (g,), half_peer).wait_recv()
        out = (z_own[g, half] + z_rx[g].astype(F32)).astype(BF16).astype(F32)
        gate_acc[...] += jnp.sum(out * cot_sel[g], axis=1, keepdims=True)
        weighted = jnp.dot(
            sel_t, (slot_gate * out).astype(BF16), preferred_element_type=F32
        ).astype(BF16)
        for n in range(PER_GROUP):
            tok[g * PER_GROUP + n] = weighted[:, n * LANES : (n + 1) * LANES]

    up_peer, down_peer = e_peer(1), e_peer(NE - 1)

    def up_copy(q):
        return remote(up_tx.at[q], up_rx.at[q], up_sem, (q,), up_peer)

    def down_copy(q):
        return remote(down_tx.at[q], down_rx.at[q], down_sem, (q,), down_peer)

    gate_x = [remote(gate_tx, gate_xrx.at[d - 1], gx_sem, (d - 1,), x_peer(d)) for d in (2, 1, 3)]
    gate_e = [
        remote(gate_sum, gate_erx.at[d - 1], ge_sem, (d - 1,), e_peer(d)) for d in range(1, NE)
    ]
    hg_copies = [
        remote(hg_tx.at[(mx + d) % NX], hg_rx.at[d - 1], hg_sem, (d - 1,), x_peer(d))
        for d in (2, 1, 3)
    ]

    def step(s, carry):
        @pl.when(jnp.logical_and(s % PER_GROUP == 0, s < CHUNKS))
        def _():
            take_group(s // PER_GROUP)

        @pl.when(s == CHUNKS - 1)
        def _():
            per_token = jnp.sum(sel * gate_acc[:, 0:1], axis=0, keepdims=True)
            gate_tx[...] = jnp.zeros_like(gate_tx)
            gate_tx[0:1, :] = per_token * hit0
            gate_tx[1:2, :] = per_token * hit1
            for copy in gate_x:
                copy.start()

        @pl.when(s == CHUNKS + 3)
        def _():
            for copy in gate_x:
                copy.wait_recv()
            gate_sum[...] = gate_tx[...] + gate_xrx[0] + gate_xrx[1] + gate_xrx[2]
            for copy in gate_e:
                copy.start()

        q = s - HOP * ex

        @pl.when(jnp.logical_and(q >= 0, q < CHUNKS))
        def _():
            @pl.when(ex == 0)
            def _():
                up_tx[q] = tok[q]

            @pl.when(ex > 0)
            def _():
                up_copy(q).wait_recv()
                up_tx[q] = (tok[q].astype(F32) + up_rx[q].astype(F32)).astype(BF16)

            @pl.when(ex < NE - 1)
            def _():
                up_copy(q).start()

        r = s - HOP * (NE - 1 - ex)

        @pl.when(jnp.logical_and(r >= 0, r < CHUNKS))
        def _():
            @pl.when(ex == NE - 1)
            def _():
                down_tx[r] = tok[r]

            @pl.when(ex < NE - 1)
            def _():
                down_copy(r).wait_recv()
                down_tx[r] = (tok[r].astype(F32) + down_rx[r].astype(F32)).astype(BF16)

            @pl.when(ex > 0)
            def _():
                down_copy(r).start()

        @pl.when(s == FORWARD_AT)
        def _():
            for copy, onward in zip(other_y, onwards):
                copy.wait_recv()
                onward.start()

        @pl.when(s == HGRAD_AT)
        def _():
            for copy in core_copies:
                copy.wait_recv()

        for n, d in enumerate((2, 1, 3, 0)):

            @pl.when(s == HGRAD_AT + n)
            def _():
                block = (mx + d) % NX
                slots = slot_all[pl.ds(block * 4, 4)].reshape(ROWS, COLS)
                hg_tx[block] = lax.dot_general(
                    slots, weight_ref[...], NT, preferred_element_type=F32
                ).astype(BF16)
                if d:
                    hg_copies[n].start()

        for g in range(GROUPS):

            @pl.when(s == WGRAD_AT + g)
            def _():
                columns = slice(g * WIDE, (g + 1) * WIDE)
                wgrad_ref[:, columns] = jnp.dot(
                    hid_t[...],
                    slot_all[:, :, columns].reshape(NX * ROWS, WIDE),
                    preferred_element_type=F32,
                ).astype(BF16)

        return carry

    lax.fori_loop(0, STEPS, step, 0)

    for q in range(CHUNKS):
        columns = slice(q * LANES, (q + 1) * LANES)

        @pl.when(ex < NE - 1)
        def _():
            mixed_ref[:, columns] = (up_tx[q].astype(F32) + down_rx[q].astype(F32)).astype(BF16)

        @pl.when(ex == NE - 1)
        def _():
            mixed_ref[:, columns] = up_tx[q]

    for copy in hg_copies:
        copy.wait_recv()
    total = hg_tx[mx].astype(F32)
    for d in range(1, NX):
        total = total + hg_rx[d - 1].astype(F32)
    hgrad_ref[...] = total.astype(BF16)

    for copy in gate_e:
        copy.wait_recv()
    gates = gate_sum[...]
    for d in range(1, NE):
        gates = gates + gate_erx[d - 1]
    gate_ref[...] = gates[0:2, :]

    for copy in [*hid_copies, *hid_onward, slot_z, *own_y, *other_y, *core_copies, *to_z]:
        copy.wait_send()
    for g in range(GROUPS):
        core_copy(g).wait_send()
        for d in range(1, NY):
            row_copy(d, g).wait_send()
    for copy in [*hg_copies, *gate_x, *gate_e]:
        copy.wait_send()

    def drain(q, carry):
        @pl.when(ex < NE - 1)
        def _():
            up_copy(q).wait_send()

        @pl.when(ex > 0)
        def _():
            down_copy(q).wait_send()

        return carry

    lax.fori_loop(0, CHUNKS, drain, 0)


def write_out(*refs):
    count = (len(refs) - 1) // 2
    copies = [
        pltpu.make_async_copy(refs[n], refs[count + n], refs[-1].at[n]) for n in range(count)
    ]
    for copy in copies:
        copy.start()
    for copy in copies:
        copy.wait()


def body(expert_ids, gate_weights, hidden, down_weight, cotangent):
    vmem = pl.BlockSpec(memory_space=pltpu.VMEM)
    hbm = pl.BlockSpec(memory_space=pltpu.HBM)
    dma = pltpu.SemaphoreType.DMA
    shapes = (
        jax.ShapeDtypeStruct((TOKS, COLS), BF16),
        jax.ShapeDtypeStruct((2, TOKS), F32),
        jax.ShapeDtypeStruct((ROWS, DEPTH), BF16),
        jax.ShapeDtypeStruct((DEPTH, COLS), BF16),
    )
    operands = (expert_ids.T, gate_weights.T, hidden[0], down_weight[0], cotangent)
    operands = [pltpu.with_memory_space_constraint(each, pltpu.HBM) for each in operands]
    results = pl.pallas_call(
        kernel,
        name="layer",
        out_shape=shapes,
        in_specs=[hbm] * 5,
        out_specs=(vmem,) * 4,
        scratch_shapes=[
            pltpu.VMEM((2, TOKS), jnp.int32),
            pltpu.VMEM((2, TOKS), F32),
            pltpu.VMEM((DEPTH, COLS), BF16),
            pltpu.VMEM((TOKS, COLS), BF16),
            pltpu.VMEM((NX, ROWS, DEPTH), BF16),
            pltpu.VMEM((DEPTH, NX * ROWS), BF16),
            pltpu.VMEM((16, CAP, COLS), BF16),
            pltpu.VMEM((GROUPS, CAP, WIDE), F32),
            pltpu.VMEM((GROUPS, 2, NY, 2, CAP, WIDE), BF16),
            pltpu.VMEM((GROUPS, NY, 2, CAP, WIDE), BF16),
            pltpu.VMEM((GROUPS, NY, 2, CAP, WIDE), BF16),
            pltpu.VMEM((GROUPS, NY - 1, 2, CAP, WIDE), BF16),
            pltpu.VMEM((GROUPS, 2, CAP, WIDE), F32),
            pltpu.VMEM((GROUPS, CAP, WIDE), BF16),
            pltpu.VMEM((GROUPS, CAP, WIDE), BF16),
            pltpu.VMEM((CHUNKS, TOKS, LANES), BF16),
            pltpu.VMEM((CHUNKS, TOKS, LANES), BF16),
            pltpu.VMEM((CHUNKS, TOKS, LANES), BF16),
            pltpu.VMEM((CHUNKS, TOKS, LANES), BF16),
            pltpu.VMEM((CHUNKS, TOKS, LANES), BF16),
            pltpu.VMEM((NX, ROWS, DEPTH), BF16),
            pltpu.VMEM((NX - 1, ROWS, DEPTH), BF16),
            pltpu.VMEM((8, TOKS), F32),
            pltpu.VMEM((8, TOKS), F32),
            pltpu.VMEM((NX - 1, 8, TOKS), F32),
            pltpu.VMEM((NE - 1, 8, TOKS), F32),
            pltpu.VMEM((CAP, TOKS), F32),
            dma((5,)),
            dma((2, 6)),
            dma((2, 1)),
            dma((2, 2, NY - 1)),
            dma((2, 8)),
            dma((2, GROUPS)),
            dma((2, GROUPS, NY - 1)),
            dma((2, GROUPS)),
            dma((2, CHUNKS)),
            dma((2, CHUNKS)),
            dma((2, NX - 1)),
            dma((2, NX - 1)),
            dma((2, NE - 1)),
        ],
        compiler_params=pltpu.CompilerParams(
            collective_id=0, has_side_effects=True, vmem_limit_bytes=50 * 2**20
        ),
    )(*operands)
    results = [pltpu.with_memory_space_constraint(each, pltpu.VMEM) for each in results]
    mixed, gates, hgrad, wgrad = pl.pallas_call(
        write_out,
        name="write_out",
        out_shape=shapes,
        in_specs=[vmem] * 4,
        out_specs=(hbm,) * 4,
        scratch_shapes=[dma((4,))],
    )(*results)
    return mixed, gates.T, hgrad[None], wgrad[None]


def solution(mesh):
    in_specs = (
        P("dp", None),
        P("dp", None),
        P("expert", "mp", "dp"),
        P("expert", "dp", "mp"),
        P("dp", "mp"),
    )
    out_specs = (P("dp", "mp"), P("dp", None), P("expert", "mp", "dp"), P("expert", "dp", "mp"))
    return jax.shard_map(body, mesh=mesh, in_specs=in_specs, out_specs=out_specs, check_vma=False)
```
